1024 devices in a mesh: user: 256 (over z, y, core), item: 4 (over x).
Axes of the slice: x: 4, y: 8, z: 16, core: 2. Of those that a mesh axis runs over, the one named last changes fastest.
Arguments:
- tiles: bfloat16 [49152, 128, 128], P(('user', 'item')), may hold values from -0.046875 to 0.046875
- tile_user: int32 [49152], P(('user', 'item')), may hold values from 0 to 3
- tile_item: int32 [49152], P(('user', 'item')), may hold values from 0 to 15
- tile_count: int32 [1024], P(('user', 'item')), may hold values from 1 to 48, as said below
- user_emb: bfloat16 [131072, 128], P('user'), may hold values from -6 to 6
- item_emb: bfloat16 [8192, 128], P('item'), may hold values from -6 to 6
Outputs:
- user_out: bfloat16 [131072, 128], P('user')
- item_out: bfloat16 [8192, 128], P(('item', 'user'))
The draws below stay inside these ranges and needn't reach their ends.
Inputs may be any that keep to these rules, and one draw needn't show every extreme that they name: `tile_count`: every device has at least one live slot; some device has all 48 live.
All inputs are finite; a program needn't handle non-finite values.
Results may differ from the reference program's by a relative error of at most 0.014.
Values may be sent and summed in bfloat16 or wider, within the bound.
No kernel may reach another device: no remote copies, remote signals or barrier semaphores. Data moves between devices by JAX's collectives and lax.ppermute only.
A program may use at most 32 MiB of HBM per device.

```python
import jax
import jax.numpy as jnp
from jax import lax

DIM = 128
BLOCK = 128
UB_DEV = 4
IB_DEV = 16
TILE_DEV = 48
USERS = 131072
ITEMS = 8192
TILES = 49152
N_USER = 256
N_ITEM = 4
DEVICES = 1024


def draw_tile_count(key, part):
    key = jax.random.fold_in(key, 1)
    level = jax.random.randint(key, (DEVICES,), 0, 8)
    counts = jnp.maximum(TILE_DEV // 8, TILE_DEV * level * level // 49)
    counts = jnp.maximum(counts, 1)
    chosen = jax.random.randint(jax.random.fold_in(key, 2), (), 0, DEVICES)
    counts = jnp.where(jnp.arange(DEVICES) == chosen, TILE_DEV, counts)
    return counts.astype(jnp.int32)


def place_ends(values, own_key, smallest, largest):
    place = [jax.random.randint(jax.random.fold_in(own_key, axis), (), 0, length) for axis, length in enumerate(values.shape)]
    widest = values.shape.index(max(values.shape))
    next_to = place[:widest] + [(place[widest] + 1) % values.shape[widest]] + place[widest + 1:]
    return values.at[tuple(place)].set(smallest).at[tuple(next_to)].set(largest)


def levels(rng, extent, shards, low, largest):
    factor_of, own = 1.0, jax.random.fold_in(rng, 6)
    for dim, parts in shards:
        steps = jnp.exp(jax.random.uniform(jax.random.fold_in(own, dim), (parts,), jnp.float32, low / len(shards), largest / len(shards)))
        factor_of = factor_of * jnp.repeat(steps, extent[dim] // parts).reshape([-1 if axis == dim else 1 for axis in range(len(extent))])
    return factor_of


def scatter_about(rng, shape, spread, reach, split=(), kind=jnp.bfloat16):
    entries = jax.random.normal(rng, shape, jnp.float32) * spread
    if len(split) > 0:
        entries = levels(rng, shape, split, -0.22, 0.18) * entries
    return jnp.clip(entries, min=-reach, max=reach).astype(kind)


def setup_inputs(seed: int = 0) -> dict:
    seeds = jax.random.split(jax.random.key(seed), 7)
    return {
        "tiles": scatter_about(seeds[0], (TILES, BLOCK, BLOCK), (BLOCK * BLOCK) ** -0.5, 0.046875, ((0, 1024),)),
        "tile_user": place_ends(jax.random.randint(seeds[1], (TILES,), 0, UB_DEV), jax.random.fold_in(seeds[1], 1), 0, UB_DEV - 1).astype(jnp.int32),
        "tile_item": place_ends(jax.random.randint(seeds[2], (TILES,), 0, IB_DEV), jax.random.fold_in(seeds[2], 1), 0, IB_DEV - 1).astype(jnp.int32),
        "tile_count": draw_tile_count(jax.random.fold_in(seeds[6], 71), 0),
        "user_emb": scatter_about(seeds[4], (USERS, DIM), 1.0, 6.0, ((0, 256),)),
        "item_emb": scatter_about(seeds[5], (ITEMS, DIM), 1.0, 6.0, ((0, 4),)),
    }


def propagate(tiles, tile_user, tile_item, tile_count, user_src, item_src):
    tiles5 = tiles.reshape(N_USER, N_ITEM, TILE_DEV, BLOCK, BLOCK)
    users3 = tile_user.reshape(N_USER, N_ITEM, TILE_DEV)
    items3 = tile_item.reshape(N_USER, N_ITEM, TILE_DEV)
    counts = tile_count.reshape(N_USER, N_ITEM)
    slots = jnp.arange(TILE_DEV, dtype=jnp.int32)
    item_blocks = item_src.reshape(N_ITEM * IB_DEV, BLOCK, DIM)
    user_blocks = user_src.reshape(N_USER, UB_DEV, BLOCK, DIM)
    offsets = (jnp.arange(N_ITEM, dtype=jnp.int32) * IB_DEV)[:, None]

    def step(item_total, index):
        tile_now = tiles5[index].astype(jnp.float32)
        live = (slots[None, :] < counts[index][:, None]).astype(jnp.float32)
        local_user = users3[index]
        local_item = items3[index]
        gathered = item_blocks[offsets + local_item].astype(jnp.float32)
        prod = jnp.einsum('jtab,jtbd->jtad', tile_now, gathered)
        pick_user = (local_user[..., None] == jnp.arange(UB_DEV, dtype=jnp.int32)).astype(jnp.float32) * live[..., None]
        user_part = jnp.einsum('jtk,jtad->kad', pick_user, prod)
        own_users = user_blocks[index][local_user].astype(jnp.float32)
        prod_back = jnp.einsum('jtab,jtad->jtbd', tile_now, own_users)
        pick_item = (local_item[..., None] == jnp.arange(IB_DEV, dtype=jnp.int32)).astype(jnp.float32) * live[..., None]
        item_part = jnp.einsum('jtk,jtbd->jkbd', pick_item, prod_back)
        return item_total + item_part, user_part

    start = jnp.zeros((N_ITEM, IB_DEV, BLOCK, DIM), jnp.float32)
    item_total, user_parts = lax.scan(step, start, jnp.arange(N_USER, dtype=jnp.int32))
    return user_parts.reshape(USERS, DIM), item_total.reshape(ITEMS, DIM)


def reference(tiles, tile_user, tile_item, tile_count, user_emb, item_emb):
    user_one, item_one = propagate(tiles, tile_user, tile_item, tile_count, user_emb, item_emb)
    user_one = user_one.astype(jnp.bfloat16)
    item_one = item_one.astype(jnp.bfloat16)
    user_two, item_two = propagate(tiles, tile_user, tile_item, tile_count, user_one, item_one)
    user_out = ((user_emb.astype(jnp.float32) + user_one.astype(jnp.float32) + user_two) / 3.0).astype(jnp.bfloat16)
    item_out = ((item_emb.astype(jnp.float32) + item_one.astype(jnp.float32) + item_two) / 3.0).astype(jnp.bfloat16)
    return user_out, item_out
```

```python
import jax
import jax.numpy as jnp
from jax import lax
from jax.experimental import pallas as pl
from jax.experimental.pallas import tpu as pltpu
from jax.sharding import Mesh, PartitionSpec as P

DIM = 128
BLOCK = 128
F32 = jnp.float32
BF16 = jnp.bfloat16

ZH, ZL, Y, CORE = 4, 4, 8, 2
GROUP = ZL * Y
AXES = ("zh", "zl", "y", "core")

VMEM = pl.BlockSpec(memory_space=pltpu.VMEM)
SMEM = pl.BlockSpec(memory_space=pltpu.SMEM)
PARAMS = pltpu.CompilerParams(vmem_limit_bytes=40 * 1024 * 1024)


def first_kernel(tu_ref, ti_ref, count_ref, tiles_ref, item_ref, r_ref, part_ref, acc_ref):
    acc_ref[...] = jnp.zeros_like(acc_ref)

    def add(s, carry):
        rows = pl.ds(pl.multiple_of(tu_ref[s] * BLOCK, BLOCK), BLOCK)
        cols = pl.ds(pl.multiple_of(ti_ref[s] * BLOCK, BLOCK), BLOCK)
        acc_ref[rows, cols] += tiles_ref[s].astype(F32)
        return carry

    lax.fori_loop(0, count_ref[0], add, 0)
    r_ref[...] = acc_ref[...].astype(BF16)
    part = jnp.dot(r_ref[...], item_ref[...], preferred_element_type=F32).astype(BF16)
    for k in range(part_ref.shape[0]):
        part_ref[k] = part


def first_call(tile_user, tile_item, tile_count, tiles, item_emb, copies, users):
    items = item_emb.shape[0]
    return pl.pallas_call(
        first_kernel,
        out_shape=(
            jax.ShapeDtypeStruct((users, items), BF16),
            jax.ShapeDtypeStruct((copies, users, DIM), BF16),
        ),
        in_specs=[SMEM, SMEM, SMEM, VMEM, VMEM],
        out_specs=(VMEM, VMEM),
        scratch_shapes=[pltpu.VMEM((users, items), F32)],
        compiler_params=PARAMS,
        name="first",
    )(tile_user, tile_item, tile_count, tiles, item_emb)


def second_kernel(core_ref, r_ref, parts_ref, user_ref, one_ref, keep_ref, send_ref, two_ref):
    total = parts_ref[0].astype(F32)
    for k in range(1, parts_ref.shape[0]):
        total += parts_ref[k].astype(F32)
    one = total.astype(BF16)
    one_ref[...] = one
    both = jnp.concatenate([user_ref[...], one], axis=1)
    core = core_ref[0]
    half = ZH * ZL * BLOCK // CORE
    dims = (((0,), (0,)), ((), ()))
    out = lax.dot_general(r_ref[...], both, dims, preferred_element_type=F32)
    first = out[:, :DIM]
    two_ref[0] = first[:half].reshape(half, DIM)
    two_ref[1] = first[half:].reshape(half, DIM)
    for ref, side in ((keep_ref, core), (send_ref, 1 - core)):
        ref[:, 0] = two_ref[side].astype(BF16).reshape(GROUP, half // GROUP, DIM)
    second = out[:, DIM:].reshape(ZH, ZL, Y, CORE, 8, DIM)
    for zl in range(ZL):
        for y in range(Y):
            for c in range(CORE):
                two_ref[c, pl.ds((zl * Y + y) * 32, 32)] = jnp.concatenate(
                    [second[zh, zl, y, c] for zh in range(ZH)], axis=0
                )
    for ref, side in ((keep_ref, core), (send_ref, 1 - core)):
        ref[:, 1] = two_ref[side].astype(BF16).reshape(GROUP, half // GROUP, DIM)


def second_call(core, r, parts, user_emb):
    users, items = r.shape
    half = items // CORE
    piece = jax.ShapeDtypeStruct((GROUP, 2, half // GROUP, DIM), BF16)
    return pl.pallas_call(
        second_kernel,
        out_shape=(jax.ShapeDtypeStruct((users, DIM), BF16), piece, piece),
        in_specs=[SMEM, VMEM, VMEM, VMEM],
        out_specs=(VMEM, VMEM, VMEM),
        scratch_shapes=[pltpu.VMEM((CORE, half, DIM), F32)],
        compiler_params=PARAMS,
        name="second",
    )(core, r, parts, user_emb)


def third_kernel(at_ref, r_ref, one_ref, emb_ref, two_ref, part_ref, out_ref):
    part = jnp.dot(r_ref[...], one_ref[...], preferred_element_type=F32).astype(BF16)
    for k in range(part_ref.shape[0]):
        part_ref[k] = part
    start = pl.multiple_of(at_ref[0] * 16, 16)
    pair = one_ref[pl.ds(start, 16)].astype(F32) + emb_ref[pl.ds(start, 16)].astype(F32)
    mine = jnp.where(at_ref[1] == 0, pair[:8], pair[8:])
    out_ref[...] = ((mine + two_ref[...]) / 3.0).astype(BF16)


def third_call(at, r, item_one, item_emb, item_two, copies):
    users, items = r.shape
    return pl.pallas_call(
        third_kernel,
        out_shape=(
            jax.ShapeDtypeStruct((copies, users, DIM), BF16),
            jax.ShapeDtypeStruct((8, DIM), BF16),
        ),
        in_specs=[SMEM, VMEM, VMEM, VMEM, VMEM],
        out_specs=(VMEM, VMEM),
        compiler_params=PARAMS,
        name="third",
    )(at, r, item_one, item_emb, item_two)


def swap(x, axis):
    return lax.all_to_all(x, axis, 0, 0, tiled=True)


def per_device(tiles, tile_user, tile_item, tile_count, user_emb, item_emb):
    copies = lax.axis_size("item")
    users = user_emb.shape[0]
    core = lax.axis_index("core")
    r, part = first_call(tile_user, tile_item, tile_count, tiles, item_emb, copies, users)
    parts = swap(part, "item")
    user_one, keep, send = second_call(core[None], r, parts, user_emb)
    other = lax.ppermute(send, "core", [(0, 1), (1, 0)])
    chip = (keep.astype(F32) + other.astype(F32)).astype(BF16)
    got = swap(chip, ("zl", "y"))
    both = got.astype(F32).sum(axis=0).astype(BF16)
    wide = jnp.broadcast_to(both[0][None], (ZH, 32, DIM))
    got = swap(jnp.concatenate([wide, both[1].reshape(ZH, 8, DIM)], axis=1), "zh")
    total = got.astype(F32).sum(axis=0)
    mine = total[:32].astype(BF16)
    half = swap(jnp.broadcast_to(mine[None], (GROUP, 32, DIM)), ("zl", "y"))
    item_one = lax.all_gather(half.reshape(GROUP * 32, DIM), "core", axis=0, tiled=True)
    block = (lax.axis_index("zh") * ZL + lax.axis_index("zl")) * Y + lax.axis_index("y")
    at = jnp.stack([block, core]).astype(jnp.int32)
    part, item_out = third_call(at, r, item_one, item_emb, total[32:], copies)
    parts = swap(part, "item")
    user_two = parts.astype(F32).sum(axis=0)
    user_out = ((user_emb.astype(F32) + user_one.astype(F32) + user_two) / 3.0).astype(BF16)
    return user_out, item_out


def solution(mesh):
    fine = Mesh(mesh.devices.reshape(ZH, ZL, Y, CORE, -1), AXES + ("item",))
    every = P(AXES + ("item",))
    in_specs = (every, every, every, every, P(AXES, None), P("item", None))
    out_specs = (P(AXES, None), P(("item",) + AXES, None))
    return jax.shard_map(
        per_device, mesh=fine, in_specs=in_specs, out_specs=out_specs, check_vma=False
    )
```

```python
import jax
import jax.numpy as jnp
from jax import lax
from jax.experimental import pallas as pl
from jax.experimental.pallas import tpu as pltpu
from jax.sharding import Mesh, PartitionSpec as P

DIM = 128
BLOCK = 128
F32 = jnp.float32
BF16 = jnp.bfloat16

ZH, ZL, Y, CORE = 8, 2, 8, 2
GROUP = ZL * Y
AXES = ("zh", "zl", "y", "core")

VMEM = pl.BlockSpec(memory_space=pltpu.VMEM)
SMEM = pl.BlockSpec(memory_space=pltpu.SMEM)
HBM = pl.BlockSpec(memory_space=pltpu.HBM)
PARAMS = pltpu.CompilerParams(vmem_limit_bytes=32 * 1024 * 1024)
FIRST_DIMS = (((0,), (0,)), ((), ()))


def first_kernel(count_ref, tu_hbm, ti_hbm, tiles_hbm, item_hbm, r_ref, part_ref,
                 tu_ref, ti_ref, head_ref, next_ref, twice_ref,
                 tiles_ref, item_ref, sems):
    slots = tiles_hbm.shape[0]
    row_blocks, col_blocks = r_ref.shape[0] // BLOCK, r_ref.shape[1] // BLOCK
    small = [
        pltpu.make_async_copy(tu_hbm, tu_ref, sems.at[0]),
        pltpu.make_async_copy(ti_hbm, ti_ref, sems.at[1]),
    ]
    tiles = pltpu.make_async_copy(tiles_hbm, tiles_ref.at[pl.ds(0, slots)], sems.at[2])
    items = pltpu.make_async_copy(item_hbm, item_ref, sems.at[3])
    for copy in small + [tiles, items]:
        copy.start()
    tiles_ref[slots] = jnp.zeros((BLOCK, BLOCK), BF16)
    for block in range(row_blocks * col_blocks):
        head_ref[block] = slots
    next_ref[slots] = -1
    for copy in small:
        copy.wait()

    def place(s, found):
        block = tu_ref[s] * col_blocks + ti_ref[s]
        before = head_ref[block]
        again = next_ref[before] == slots
        next_ref[s] = before
        head_ref[block] = s
        twice_ref[found] = block
        return found + again.astype(jnp.int32)

    found = lax.fori_loop(0, count_ref[0], place, jnp.int32(0))
    tiles.wait()
    for u in range(row_blocks):
        for i in range(col_blocks):
            tile = tiles_ref[head_ref[u * col_blocks + i]]
            r_ref[u * BLOCK : (u + 1) * BLOCK, i * BLOCK : (i + 1) * BLOCK] = tile

    def gather(k, carry):
        block = twice_ref[k]
        start = head_ref[block]
        _, total = lax.while_loop(
            lambda at: at[0] != slots,
            lambda at: (next_ref[at[0]], at[1] + tiles_ref[at[0]].astype(F32)),
            (next_ref[start], tiles_ref[start].astype(F32)),
        )
        rows = pl.ds(pl.multiple_of(block // col_blocks * BLOCK, BLOCK), BLOCK)
        cols = pl.ds(pl.multiple_of(block % col_blocks * BLOCK, BLOCK), BLOCK)
        r_ref[rows, cols] = total.astype(BF16)
        return carry

    lax.fori_loop(0, found, gather, 0)
    items.wait()
    part = jnp.dot(r_ref[...], item_ref[...], preferred_element_type=F32)
    part_ref[...] = part.astype(BF16)


def first_call(tile_user, tile_item, tile_count, tiles, item_emb, users):
    items, slots = item_emb.shape[0], tiles.shape[0]
    blocks = (users // BLOCK) * (items // BLOCK)
    inputs = (tile_user, tile_item, tiles, item_emb)
    return pl.pallas_call(
        first_kernel,
        out_shape=(
            jax.ShapeDtypeStruct((users, items), BF16),
            jax.ShapeDtypeStruct((users, DIM), BF16),
        ),
        in_specs=[SMEM] + [HBM] * 4,
        out_specs=(VMEM, VMEM),
        scratch_shapes=[
            pltpu.SMEM((slots,), jnp.int32),
            pltpu.SMEM((slots,), jnp.int32),
            pltpu.SMEM((blocks,), jnp.int32),
            pltpu.SMEM((slots + 1,), jnp.int32),
            pltpu.SMEM((slots + 1,), jnp.int32),
            pltpu.VMEM((slots + 1, BLOCK, BLOCK), BF16),
            pltpu.VMEM(item_emb.shape, BF16),
            pltpu.SemaphoreType.DMA((4,)),
        ],
        compiler_params=PARAMS,
        name="first",
    )(tile_count, *(pltpu.with_memory_space_constraint(x, pltpu.HBM) for x in inputs))


def second_kernel(r_ref, parts_ref, user_ref, one_ref, keep_ref, send_ref, two_ref):
    total = parts_ref[0].astype(F32)
    for k in range(1, parts_ref.shape[0]):
        total += parts_ref[k].astype(F32)
    one = total.astype(BF16)
    one_ref[...] = one
    both = jnp.concatenate([user_ref[...], one], axis=1)
    back = lax.dot_general(r_ref[...], both, FIRST_DIMS, preferred_element_type=F32)
    two_ref[:, :, 0] = back[:, :DIM].astype(BF16).reshape(CORE, GROUP, -1, DIM)
    back = back[:, DIM:].reshape(ZH, ZL, Y, CORE, 8, DIM)
    for zl in range(ZL):
        for y in range(Y):
            for c in range(CORE):
                rows = jnp.concatenate([back[zh, zl, y, c] for zh in range(ZH)], axis=0)
                two_ref[c, zl * Y + y, 1] = rows.astype(BF16)
    core = lax.axis_index("core")
    keep_ref[...] = two_ref[core]
    send_ref[...] = two_ref[1 - core]


def second_call(r, parts, user_emb):
    users, items = r.shape
    piece = jax.ShapeDtypeStruct((GROUP, 2, items // CORE // GROUP, DIM), BF16)
    return pl.pallas_call(
        second_kernel,
        out_shape=(jax.ShapeDtypeStruct((users, DIM), BF16), piece, piece),
        in_specs=[VMEM, VMEM, VMEM],
        out_specs=(VMEM, VMEM, VMEM),
        scratch_shapes=[pltpu.VMEM((CORE,) + piece.shape, BF16)],
        compiler_params=PARAMS,
        name="second",
    )(r, parts, user_emb)


def spread_kernel(got_ref, out_ref, two_ref):
    total = got_ref[0].astype(F32)
    for k in range(1, got_ref.shape[0]):
        total += got_ref[k].astype(F32)
    rows = out_ref.shape[1]
    one = total[:rows].astype(BF16)
    for k in range(out_ref.shape[0]):
        out_ref[k] = one
    two_ref[...] = total[rows : rows + two_ref.shape[0]]


def spread_call(got, rows):
    return pl.pallas_call(
        spread_kernel,
        out_shape=(
            jax.ShapeDtypeStruct((GROUP, rows, DIM), BF16),
            jax.ShapeDtypeStruct((8, DIM), F32),
        ),
        in_specs=[VMEM],
        out_specs=(VMEM, VMEM),
        compiler_params=PARAMS,
        name="spread",
    )(got)


def third_kernel(r_ref, one_ref, emb_ref, two_ref, part_ref, out_ref):
    part = jnp.dot(r_ref[...], one_ref[...], preferred_element_type=F32)
    part_ref[...] = part.astype(BF16)
    block = (lax.axis_index("zh") * ZL + lax.axis_index("zl")) * Y + lax.axis_index("y")
    rows = pl.ds(pl.multiple_of(block * 16, 16), 16)
    pair = one_ref[rows].astype(F32) + emb_ref[rows].astype(F32)
    mine = jnp.where(lax.axis_index("core") == 0, pair[:8], pair[8:])
    out_ref[...] = ((mine + two_ref[...]) / 3.0).astype(BF16)


def third_call(r, item_one, item_emb, item_two):
    users, items = r.shape
    return pl.pallas_call(
        third_kernel,
        out_shape=(
            jax.ShapeDtypeStruct((users, DIM), BF16),
            jax.ShapeDtypeStruct((8, DIM), BF16),
        ),
        in_specs=[VMEM, VMEM, VMEM, VMEM],
        out_specs=(VMEM, VMEM),
        compiler_params=PARAMS,
        name="third",
    )(r, item_one, item_emb, item_two)


def swap(x, axis):
    return lax.all_to_all(x, axis, 0, 0, tiled=True)


def add_up(x):
    return x.astype(F32).sum(axis=0)


def per_device(tiles, tile_user, tile_item, tile_count, user_emb, item_emb):
    users = user_emb.shape[0]
    r, part = first_call(tile_user, tile_item, tile_count, tiles, item_emb, users)
    user_one, keep, send = second_call(r, lax.all_gather(part, "item", axis=0), user_emb)
    other = lax.ppermute(send, "core", [(0, 1), (1, 0)])
    chip = (keep.astype(F32) + other.astype(F32)).astype(BF16)
    both = add_up(swap(chip, ("zl", "y"))).astype(BF16)
    rows = both.shape[1]
    wide = jnp.broadcast_to(both[0][None], (ZH, rows, DIM))
    got = swap(jnp.concatenate([wide, both[1].reshape(ZH, -1, DIM)], axis=1), "zh")
    spread, item_two = spread_call(got, rows)
    half = swap(spread, ("zl", "y"))
    item_one = lax.all_gather(half.reshape(-1, DIM), "core", axis=0, tiled=True)
    part, item_out = third_call(r, item_one, item_emb, item_two)
    parts = lax.all_gather(part, "item", axis=0)
    user_out = ((user_emb.astype(F32) + user_one.astype(F32) + add_up(parts)) / 3.0).astype(BF16)
    return user_out, item_out


def solution(mesh):
    fine = Mesh(mesh.devices.reshape(ZH, ZL, Y, CORE, -1), AXES + ("item",))
    every = P(AXES + ("item",))
    in_specs = (every, every, every, every, P(AXES, None), P("item", None))
    out_specs = (P(AXES, None), P(("item",) + AXES, None))
    return jax.shard_map(
        per_device, mesh=fine, in_specs=in_specs, out_specs=out_specs, check_vma=False
    )
```

```python
import jax
import jax.numpy as jnp
from jax import lax
from jax.experimental import pallas as pl
from jax.experimental.pallas import tpu as pltpu
from jax.sharding import Mesh, PartitionSpec as P

DIM = 128
BLOCK = 128
F32 = jnp.float32
BF16 = jnp.bfloat16

ZH, ZL, Y, CORE = 8, 2, 8, 2
GROUP = ZL * Y
AXES = ("zh", "zl", "y", "core")

VMEM = pl.BlockSpec(memory_space=pltpu.VMEM)
SMEM = pl.BlockSpec(memory_space=pltpu.SMEM)
HBM = pl.BlockSpec(memory_space=pltpu.HBM)
PARAMS = pltpu.CompilerParams(vmem_limit_bytes=32 * 1024 * 1024)
FIRST_DIMS = (((0,), (0,)), ((), ()))


def first_kernel(count_ref, tu_hbm, ti_hbm, tiles_hbm, item_hbm, user_hbm, r_ref, part_ref, user_ref,
                 tu_ref, ti_ref, head_ref, next_ref, twice_ref,
                 tiles_ref, item_ref, sems):
    slots = tiles_hbm.shape[0]
    row_blocks, col_blocks = r_ref.shape[0] // BLOCK, r_ref.shape[1] // BLOCK
    small = [
        pltpu.make_async_copy(tu_hbm, tu_ref, sems.at[0]),
        pltpu.make_async_copy(ti_hbm, ti_ref, sems.at[1]),
    ]
    tiles = pltpu.make_async_copy(tiles_hbm, tiles_ref.at[pl.ds(0, slots)], sems.at[2])
    items = pltpu.make_async_copy(item_hbm, item_ref, sems.at[3])
    own = pltpu.make_async_copy(user_hbm, user_ref, sems.at[4])
    for copy in small + [tiles, items, own]:
        copy.start()
    tiles_ref[slots] = jnp.zeros((BLOCK, BLOCK), BF16)
    for block in range(row_blocks * col_blocks):
        head_ref[block] = slots
    next_ref[slots] = -1
    for copy in small:
        copy.wait()

    def place(s, found):
        block = tu_ref[s] * col_blocks + ti_ref[s]
        before = head_ref[block]
        again = next_ref[before] == slots
        next_ref[s] = before
        head_ref[block] = s
        twice_ref[found] = block
        return found + again.astype(jnp.int32)

    found = lax.fori_loop(0, count_ref[0], place, jnp.int32(0))
    tiles.wait()
    for u in range(row_blocks):
        for i in range(col_blocks):
            tile = tiles_ref[head_ref[u * col_blocks + i]]
            r_ref[u * BLOCK : (u + 1) * BLOCK, i * BLOCK : (i + 1) * BLOCK] = tile

    def gather(k, carry):
        block = twice_ref[k]
        start = head_ref[block]
        _, total = lax.while_loop(
            lambda at: at[0] != slots,
            lambda at: (next_ref[at[0]], at[1] + tiles_ref[at[0]].astype(F32)),
            (next_ref[start], tiles_ref[start].astype(F32)),
        )
        rows = pl.ds(pl.multiple_of(block // col_blocks * BLOCK, BLOCK), BLOCK)
        cols = pl.ds(pl.multiple_of(block % col_blocks * BLOCK, BLOCK), BLOCK)
        r_ref[rows, cols] = total.astype(BF16)
        return carry

    lax.fori_loop(0, found, gather, 0)
    items.wait()
    own.wait()
    part = jnp.dot(r_ref[...], item_ref[...], preferred_element_type=F32)
    part_ref[...] = part.astype(BF16)


def first_call(tile_user, tile_item, tile_count, tiles, item_emb, user_emb):
    items, slots = item_emb.shape[0], tiles.shape[0]
    users = user_emb.shape[0]
    blocks = (users // BLOCK) * (items // BLOCK)
    inputs = (tile_user, tile_item, tiles, item_emb, user_emb)
    return pl.pallas_call(
        first_kernel,
        out_shape=(
            jax.ShapeDtypeStruct((users, items), BF16),
            jax.ShapeDtypeStruct((users, DIM), BF16),
            jax.ShapeDtypeStruct((users, DIM), BF16),
        ),
        in_specs=[SMEM] + [HBM] * 5,
        out_specs=(VMEM, VMEM, VMEM),
        scratch_shapes=[
            pltpu.SMEM((slots,), jnp.int32),
            pltpu.SMEM((slots,), jnp.int32),
            pltpu.SMEM((blocks,), jnp.int32),
            pltpu.SMEM((slots + 1,), jnp.int32),
            pltpu.SMEM((slots + 1,), jnp.int32),
            pltpu.VMEM((slots + 1, BLOCK, BLOCK), BF16),
            pltpu.VMEM(item_emb.shape, BF16),
            pltpu.SemaphoreType.DMA((5,)),
        ],
        compiler_params=PARAMS,
        name="first",
    )(tile_count, *(pltpu.with_memory_space_constraint(x, pltpu.HBM) for x in inputs))


def back_kernel(r_ref, user_ref, keep_ref, send_ref, two_ref):
    back = lax.dot_general(r_ref[...], user_ref[...], FIRST_DIMS, preferred_element_type=F32)
    two_ref[...] = back.astype(BF16).reshape(two_ref.shape)
    core = lax.axis_index("core")
    keep_ref[...] = two_ref[core]
    send_ref[...] = two_ref[1 - core]


def back_call(r, user_emb):
    piece = jax.ShapeDtypeStruct((GROUP, r.shape[1] // CORE // GROUP, DIM), BF16)
    return pl.pallas_call(
        back_kernel,
        out_shape=(piece, piece),
        in_specs=[VMEM, VMEM],
        out_specs=(VMEM, VMEM),
        scratch_shapes=[pltpu.VMEM((CORE,) + piece.shape, BF16)],
        compiler_params=PARAMS,
        name="back",
    )(r, user_emb)


def second_kernel(r_ref, parts_ref, one_hbm, keep_ref, send_ref, two_ref, one_ref, sem):
    total = parts_ref[0].astype(F32)
    for k in range(1, parts_ref.shape[0]):
        total += parts_ref[k].astype(F32)
    one = total.astype(BF16)
    one_ref[...] = one
    copy = pltpu.make_async_copy(one_ref, one_hbm, sem)
    copy.start()
    back = lax.dot_general(r_ref[...], one, FIRST_DIMS, preferred_element_type=F32)
    back = back.reshape(ZH, ZL, Y, CORE, 8, DIM)
    for zl in range(ZL):
        for y in range(Y):
            for c in range(CORE):
                rows = jnp.concatenate([back[zh, zl, y, c] for zh in range(ZH)], axis=0)
                two_ref[c, zl * Y + y] = rows.astype(BF16)
    core = lax.axis_index("core")
    keep_ref[...] = two_ref[core]
    send_ref[...] = two_ref[1 - core]
    copy.wait()


def second_call(r, parts):
    users, items = r.shape
    piece = jax.ShapeDtypeStruct((GROUP, items // CORE // GROUP, DIM), BF16)
    return pl.pallas_call(
        second_kernel,
        out_shape=(pltpu.HBM((users, DIM), BF16), piece, piece),
        in_specs=[VMEM, VMEM],
        out_specs=(HBM, VMEM, VMEM),
        scratch_shapes=[
            pltpu.VMEM((CORE,) + piece.shape, BF16),
            pltpu.VMEM((users, DIM), BF16),
            pltpu.SemaphoreType.DMA,
        ],
        compiler_params=PARAMS,
        name="second",
    )(r, parts)


def spread_kernel(got_ref, keep_ref, sent_ref, out_ref):
    total = got_ref[0].astype(F32)
    for k in range(1, got_ref.shape[0]):
        total += got_ref[k].astype(F32)
    total = total.astype(BF16)
    for k in range(out_ref.shape[0]):
        out_ref[k, 0] = total
    other = sent_ref[1 - lax.axis_index("core")].astype(F32)
    out_ref[:, 1] = (keep_ref[...].astype(F32) + other).astype(BF16)


def spread_call(got, keep, sent):
    return pl.pallas_call(
        spread_kernel,
        out_shape=jax.ShapeDtypeStruct((GROUP, 2) + got.shape[1:], BF16),
        in_specs=[VMEM, VMEM, VMEM],
        out_specs=VMEM,
        compiler_params=PARAMS,
        name="spread",
    )(got, keep, sent)


def third_kernel(r_ref, one_ref, emb_ref, part_ref, out_ref):
    part = jnp.dot(r_ref[...], one_ref[...], preferred_element_type=F32)
    part_ref[...] = part.astype(BF16)
    block = (lax.axis_index("zh") * ZL + lax.axis_index("zl")) * Y + lax.axis_index("y")
    rows = pl.ds(pl.multiple_of(block * 16, 16), 16)
    pair = one_ref[rows].astype(F32) + emb_ref[rows].astype(F32)
    mine = jnp.where(lax.axis_index("core") == 0, pair[:8], pair[8:])
    out_ref[...] = mine


def third_call(r, item_one, item_emb):
    users, items = r.shape
    return pl.pallas_call(
        third_kernel,
        out_shape=(
            jax.ShapeDtypeStruct((users, DIM), BF16),
            jax.ShapeDtypeStruct((8, DIM), F32),
        ),
        in_specs=[VMEM, VMEM, VMEM],
        out_specs=(VMEM, VMEM),
        compiler_params=PARAMS,
        name="third",
    )(r, item_one, item_emb)


def last_kernel(user_ref, one_ref, parts_ref, base_ref, two_ref, user_out_ref, item_out_ref):
    total = user_ref[...].astype(F32) + one_ref[...].astype(F32)
    for k in range(parts_ref.shape[0]):
        total += parts_ref[k].astype(F32)
    user_out_ref[...] = (total / 3.0).astype(BF16)
    two = two_ref[...].astype(F32).sum(axis=0)
    item_out_ref[...] = ((base_ref[...] + two) / 3.0).astype(BF16)


def last_call(user_emb, user_one, parts, base, two):
    return pl.pallas_call(
        last_kernel,
        out_shape=(
            jax.ShapeDtypeStruct(user_emb.shape, BF16),
            jax.ShapeDtypeStruct(base.shape, BF16),
        ),
        in_specs=[VMEM] * 5,
        out_specs=(VMEM, VMEM),
        compiler_params=PARAMS,
        name="last",
    )(user_emb, user_one, parts, base, two)


def swap(x, axis):
    return lax.all_to_all(x, axis, 0, 0, tiled=True)


def add_up(x):
    return x.astype(F32).sum(axis=0)


def per_device(tiles, tile_user, tile_item, tile_count, user_emb, item_emb):
    r, part, own = first_call(tile_user, tile_item, tile_count, tiles, item_emb, user_emb)
    keep, send = back_call(r, own)
    other = lax.ppermute(send, "core", [(0, 1), (1, 0)])
    chip = (keep.astype(F32) + other.astype(F32)).astype(BF16)
    chip, part = lax.optimization_barrier((chip, part))
    got = swap(chip, ("zl", "y"))
    parts = lax.all_gather(part, "item", axis=0)

    got, parts = lax.optimization_barrier((got, parts))
    rows = add_up(got).astype(BF16)
    wide = jnp.broadcast_to(rows[None], (ZH,) + rows.shape)
    wide, parts = lax.optimization_barrier((wide, parts))
    got = swap(wide, "zh")
    user_one, keep, send = second_call(r, parts)
    sent = lax.all_gather(send, "core", axis=0)
    got = swap(spread_call(got, keep, sent), ("zl", "y"))

    two = add_up(got[:, 1]).astype(BF16)
    half, two = lax.optimization_barrier((got[:, 0], two))
    two = swap(two.reshape(ZH, -1, DIM), "zh")
    item_one = lax.all_gather(half.reshape(-1, DIM), "core", axis=0, tiled=True)
    part, base = third_call(r, item_one, item_emb)
    parts = lax.all_gather(part, "item", axis=0)
    return last_call(user_emb, user_one, parts, base, two)


def solution(mesh):
    fine = Mesh(mesh.devices.reshape(ZH, ZL, Y, CORE, -1), AXES + ("item",))
    every = P(AXES + ("item",))
    in_specs = (every, every, every, every, P(AXES, None), P("item", None))
    out_specs = (P(AXES, None), P(("item",) + AXES, None))
    return jax.shard_map(
        per_device, mesh=fine, in_specs=in_specs, out_specs=out_specs, check_vma=False
    )
```

```python
import jax
import jax.numpy as jnp
from jax import lax
from jax.experimental import pallas as pl
from jax.experimental.pallas import tpu as pltpu
from jax.sharding import Mesh, PartitionSpec as P

DIM = 128
BLOCK = 128
F32 = jnp.float32
BF16 = jnp.bfloat16

ZH, ZL, Y, CORE = 8, 2, 8, 2
GROUP = ZL * Y
AXES = ("zh", "zl", "y", "core")

VMEM = pl.BlockSpec(memory_space=pltpu.VMEM)
SMEM = pl.BlockSpec(memory_space=pltpu.SMEM)
HBM = pl.BlockSpec(memory_space=pltpu.HBM)
PARAMS = pltpu.CompilerParams(vmem_limit_bytes=32 * 1024 * 1024)
FIRST_DIMS = (((0,), (0,)), ((), ()))


def first_kernel(count_ref, tu_hbm, ti_hbm, tiles_hbm, item_hbm, user_hbm, r_ref, item_ref, user_ref,
                 tu_ref, ti_ref, head_ref, next_ref, twice_ref,
                 tiles_ref, sems):
    slots = tiles_hbm.shape[0]
    row_blocks, col_blocks = r_ref.shape[0] // BLOCK, r_ref.shape[1] // BLOCK
    small = [
        pltpu.make_async_copy(tu_hbm, tu_ref, sems.at[0]),
        pltpu.make_async_copy(ti_hbm, ti_ref, sems.at[1]),
    ]
    tiles = pltpu.make_async_copy(tiles_hbm, tiles_ref.at[pl.ds(0, slots)], sems.at[2])
    items = pltpu.make_async_copy(item_hbm, item_ref, sems.at[3])
    own = pltpu.make_async_copy(user_hbm, user_ref, sems.at[4])
    for copy in small + [tiles, items, own]:
        copy.start()
    tiles_ref[slots] = jnp.zeros((BLOCK, BLOCK), BF16)
    for block in range(row_blocks * col_blocks):
        head_ref[block] = slots
    next_ref[slots] = -1
    for copy in small:
        copy.wait()

    def place(s, found):
        block = tu_ref[s] * col_blocks + ti_ref[s]
        before = head_ref[block]
        again = next_ref[before] == slots
        next_ref[s] = before
        head_ref[block] = s
        twice_ref[found] = block
        return found + again.astype(jnp.int32)

    found = lax.fori_loop(0, count_ref[0], place, jnp.int32(0))
    tiles.wait()
    for u in range(row_blocks):
        for i in range(col_blocks):
            tile = tiles_ref[head_ref[u * col_blocks + i]]
            r_ref[u * BLOCK : (u + 1) * BLOCK, i * BLOCK : (i + 1) * BLOCK] = tile

    def gather(k, carry):
        block = twice_ref[k]
        start = head_ref[block]
        _, total = lax.while_loop(
            lambda at: at[0] != slots,
            lambda at: (next_ref[at[0]], at[1] + tiles_ref[at[0]].astype(F32)),
            (next_ref[start], tiles_ref[start].astype(F32)),
        )
        rows = pl.ds(pl.multiple_of(block // col_blocks * BLOCK, BLOCK), BLOCK)
        cols = pl.ds(pl.multiple_of(block % col_blocks * BLOCK, BLOCK), BLOCK)
        r_ref[rows, cols] = total.astype(BF16)
        return carry

    lax.fori_loop(0, found, gather, 0)
    items.wait()
    own.wait()


def first_call(tile_user, tile_item, tile_count, tiles, item_emb, user_emb):
    items, slots = item_emb.shape[0], tiles.shape[0]
    users = user_emb.shape[0]
    blocks = (users // BLOCK) * (items // BLOCK)
    inputs = (tile_user, tile_item, tiles, item_emb, user_emb)
    return pl.pallas_call(
        first_kernel,
        out_shape=(
            jax.ShapeDtypeStruct((users, items), BF16),
            jax.ShapeDtypeStruct((items, DIM), BF16),
            jax.ShapeDtypeStruct((users, DIM), BF16),
        ),
        in_specs=[SMEM] + [HBM] * 5,
        out_specs=(VMEM, VMEM, VMEM),
        scratch_shapes=[
            pltpu.SMEM((slots,), jnp.int32),
            pltpu.SMEM((slots,), jnp.int32),
            pltpu.SMEM((blocks,), jnp.int32),
            pltpu.SMEM((slots + 1,), jnp.int32),
            pltpu.SMEM((slots + 1,), jnp.int32),
            pltpu.VMEM((slots + 1, BLOCK, BLOCK), BF16),
            pltpu.SemaphoreType.DMA((5,)),
        ],
        compiler_params=PARAMS,
        name="first",
    )(tile_count, *(pltpu.with_memory_space_constraint(x, pltpu.HBM) for x in inputs))


def part_kernel(r_ref, item_ref, part_ref):
    part = jnp.dot(r_ref[...], item_ref[...], preferred_element_type=F32)
    part_ref[...] = part.astype(BF16)


def part_call(r, item_emb):
    return pl.pallas_call(
        part_kernel,
        out_shape=jax.ShapeDtypeStruct((r.shape[0], DIM), BF16),
        in_specs=[VMEM, VMEM],
        out_specs=VMEM,
        compiler_params=PARAMS,
        name="part",
    )(r, item_emb)


def back_kernel(r_ref, user_ref, keep_ref, send_ref, two_ref):
    back = lax.dot_general(r_ref[...], user_ref[...], FIRST_DIMS, preferred_element_type=F32)
    two_ref[...] = back.astype(BF16).reshape(two_ref.shape)
    core = lax.axis_index("core")
    keep_ref[...] = two_ref[core]
    send_ref[...] = two_ref[1 - core]


def back_call(r, user_emb):
    piece = jax.ShapeDtypeStruct((GROUP, r.shape[1] // CORE // GROUP, DIM), BF16)
    return pl.pallas_call(
        back_kernel,
        out_shape=(piece, piece),
        in_specs=[VMEM, VMEM],
        out_specs=(VMEM, VMEM),
        scratch_shapes=[pltpu.VMEM((CORE,) + piece.shape, BF16)],
        compiler_params=PARAMS,
        name="back",
    )(r, user_emb)


def second_kernel(r_ref, parts_ref, one_hbm, keep_ref, send_ref, two_ref, one_ref, sem):
    total = parts_ref[0].astype(F32)
    for k in range(1, parts_ref.shape[0]):
        total += parts_ref[k].astype(F32)
    one = total.astype(BF16)
    one_ref[...] = one
    copy = pltpu.make_async_copy(one_ref, one_hbm, sem)
    copy.start()
    back = lax.dot_general(r_ref[...], one, FIRST_DIMS, preferred_element_type=F32)
    back = back.reshape(ZH, ZL, Y, CORE, 8, DIM)
    for zl in range(ZL):
        for y in range(Y):
            for c in range(CORE):
                rows = jnp.concatenate([back[zh, zl, y, c] for zh in range(ZH)], axis=0)
                two_ref[c, zl * Y + y] = rows.astype(BF16)
    core = lax.axis_index("core")
    keep_ref[...] = two_ref[core]
    send_ref[...] = two_ref[1 - core]
    copy.wait()


def second_call(r, parts):
    users, items = r.shape
    piece = jax.ShapeDtypeStruct((GROUP, items // CORE // GROUP, DIM), BF16)
    return pl.pallas_call(
        second_kernel,
        out_shape=(pltpu.HBM((users, DIM), BF16), piece, piece),
        in_specs=[VMEM, VMEM],
        out_specs=(HBM, VMEM, VMEM),
        scratch_shapes=[
            pltpu.VMEM((CORE,) + piece.shape, BF16),
            pltpu.VMEM((users, DIM), BF16),
            pltpu.SemaphoreType.DMA,
        ],
        compiler_params=PARAMS,
        name="second",
    )(r, parts)


def spread_kernel(got_ref, keep_ref, sent_ref, out_ref):
    total = got_ref[0].astype(F32)
    for k in range(1, got_ref.shape[0]):
        total += got_ref[k].astype(F32)
    total = total.astype(BF16)
    for k in range(out_ref.shape[0]):
        out_ref[k, 0] = total
    other = sent_ref[1 - lax.axis_index("core")].astype(F32)
    out_ref[:, 1] = (keep_ref[...].astype(F32) + other).astype(BF16)


def spread_call(got, keep, sent):
    return pl.pallas_call(
        spread_kernel,
        out_shape=jax.ShapeDtypeStruct((GROUP, 2) + got.shape[1:], BF16),
        in_specs=[VMEM, VMEM, VMEM],
        out_specs=VMEM,
        compiler_params=PARAMS,
        name="spread",
    )(got, keep, sent)


def third_kernel(r_ref, one_ref, emb_ref, part_ref, out_ref):
    part = jnp.dot(r_ref[...], one_ref[...], preferred_element_type=F32)
    part_ref[...] = part.astype(BF16)
    block = (lax.axis_index("zh") * ZL + lax.axis_index("zl")) * Y + lax.axis_index("y")
    rows = pl.ds(pl.multiple_of(block * 16, 16), 16)
    pair = one_ref[rows].astype(F32) + emb_ref[rows].astype(F32)
    mine = jnp.where(lax.axis_index("core") == 0, pair[:8], pair[8:])
    out_ref[...] = mine


def third_call(r, item_one, item_emb):
    users, items = r.shape
    return pl.pallas_call(
        third_kernel,
        out_shape=(
            jax.ShapeDtypeStruct((users, DIM), BF16),
            jax.ShapeDtypeStruct((8, DIM), F32),
        ),
        in_specs=[VMEM, VMEM, VMEM],
        out_specs=(VMEM, VMEM),
        compiler_params=PARAMS,
        name="third",
    )(r, item_one, item_emb)


def last_kernel(user_ref, one_ref, parts_ref, base_ref, two_ref, user_out_ref, item_out_ref):
    total = user_ref[...].astype(F32) + one_ref[...].astype(F32)
    for k in range(parts_ref.shape[0]):
        total += parts_ref[k].astype(F32)
    user_out_ref[...] = (total / 3.0).astype(BF16)
    two = two_ref[...].astype(F32).sum(axis=0)
    item_out_ref[...] = ((base_ref[...] + two) / 3.0).astype(BF16)


def last_call(user_emb, user_one, parts, base, two):
    return pl.pallas_call(
        last_kernel,
        out_shape=(
            jax.ShapeDtypeStruct(user_emb.shape, BF16),
            jax.ShapeDtypeStruct(base.shape, BF16),
        ),
        in_specs=[VMEM] * 5,
        out_specs=(VMEM, VMEM),
        compiler_params=PARAMS,
        name="last",
    )(user_emb, user_one, parts, base, two)


def swap(x, axis):
    return lax.all_to_all(x, axis, 0, 0, tiled=True)


def add_up(x):
    return x.astype(F32).sum(axis=0)


def per_device(tiles, tile_user, tile_item, tile_count, user_emb, item_emb):
    r, items, own = first_call(tile_user, tile_item, tile_count, tiles, item_emb, user_emb)
    keep, send = back_call(r, own)
    items, send = lax.optimization_barrier((items, send))
    part = part_call(r, items)
    other = lax.ppermute(send, "core", [(0, 1), (1, 0)])
    chip = (keep.astype(F32) + other.astype(F32)).astype(BF16)
    chip, part = lax.optimization_barrier((chip, part))
    got = swap(chip, ("zl", "y"))
    parts = lax.all_gather(part, "item", axis=0)

    got, parts = lax.optimization_barrier((got, parts))
    rows = add_up(got).astype(BF16)
    wide = jnp.broadcast_to(rows[None], (ZH,) + rows.shape)
    wide, parts = lax.optimization_barrier((wide, parts))
    got = swap(wide, "zh")
    user_one, keep, send = second_call(r, parts)
    sent = lax.all_gather(send, "core", axis=0)
    got = swap(spread_call(got, keep, sent), ("zl", "y"))

    two = add_up(got[:, 1]).astype(BF16)
    half = got[:, 0]
    item_one = lax.all_gather(half.reshape(-1, DIM), "core", axis=0, tiled=True)
    part, base = third_call(r, item_one, item_emb)
    two, part = lax.optimization_barrier((two, part))
    two = swap(two.reshape(ZH, -1, DIM), "zh")
    parts = lax.all_gather(part, "item", axis=0)
    return last_call(user_emb, user_one, parts, base, two)


def solution(mesh):
    fine = Mesh(mesh.devices.reshape(ZH, ZL, Y, CORE, -1), AXES + ("item",))
    every = P(AXES + ("item",))
    in_specs = (every, every, every, every, P(AXES, None), P("item", None))
    out_specs = (P(AXES, None), P(("item",) + AXES, None))
    return jax.shard_map(
        per_device, mesh=fine, in_specs=in_specs, out_specs=out_specs, check_vma=False
    )
```

```python
import jax
import jax.numpy as jnp
from jax import lax
from jax.experimental import pallas as pl
from jax.experimental.pallas import tpu as pltpu
from jax.sharding import Mesh, PartitionSpec as P

DIM = 128
BLOCK = 128
F32 = jnp.float32
BF16 = jnp.bfloat16

ZH, ZL, Y, CORE = 8, 2, 8, 2
GROUP = ZL * Y
AXES = ("zh", "zl", "y", "core")

VMEM = pl.BlockSpec(memory_space=pltpu.VMEM)
SMEM = pl.BlockSpec(memory_space=pltpu.SMEM)
HBM = pl.BlockSpec(memory_space=pltpu.HBM)
PARAMS = pltpu.CompilerParams(vmem_limit_bytes=32 * 1024 * 1024)
FIRST_DIMS = (((0,), (0,)), ((), ()))


def first_kernel(count_ref, tu_hbm, ti_hbm, tiles_hbm, item_hbm, user_hbm, r_ref, item_ref, user_ref,
                 tu_ref, ti_ref, head_ref, next_ref, twice_ref,
                 tiles_ref, sems):
    slots = tiles_hbm.shape[0]
    row_blocks, col_blocks = r_ref.shape[0] // BLOCK, r_ref.shape[1] // BLOCK
    small = [
        pltpu.make_async_copy(tu_hbm, tu_ref, sems.at[0]),
        pltpu.make_async_copy(ti_hbm, ti_ref, sems.at[1]),
    ]
    tiles = pltpu.make_async_copy(tiles_hbm, tiles_ref.at[pl.ds(0, slots)], sems.at[2])
    items = pltpu.make_async_copy(item_hbm, item_ref, sems.at[3])
    own = pltpu.make_async_copy(user_hbm, user_ref, sems.at[4])
    for copy in small + [tiles, items, own]:
        copy.start()
    tiles_ref[slots] = jnp.zeros((BLOCK, BLOCK), BF16)
    for block in range(row_blocks * col_blocks):
        head_ref[block] = slots
    next_ref[slots] = -1
    for copy in small:
        copy.wait()

    def place(s, found):
        block = tu_ref[s] * col_blocks + ti_ref[s]
        before = head_ref[block]
        again = next_ref[before] == slots
        next_ref[s] = before
        head_ref[block] = s
        twice_ref[found] = block
        return found + again.astype(jnp.int32)

    found = lax.fori_loop(0, count_ref[0], place, jnp.int32(0))
    tiles.wait()
    for u in range(row_blocks):
        for i in range(col_blocks):
            tile = tiles_ref[head_ref[u * col_blocks + i]]
            r_ref[u * BLOCK : (u + 1) * BLOCK, i * BLOCK : (i + 1) * BLOCK] = tile

    def gather(k, carry):
        block = twice_ref[k]
        start = head_ref[block]
        _, total = lax.while_loop(
            lambda at: at[0] != slots,
            lambda at: (next_ref[at[0]], at[1] + tiles_ref[at[0]].astype(F32)),
            (next_ref[start], tiles_ref[start].astype(F32)),
        )
        rows = pl.ds(pl.multiple_of(block // col_blocks * BLOCK, BLOCK), BLOCK)
        cols = pl.ds(pl.multiple_of(block % col_blocks * BLOCK, BLOCK), BLOCK)
        r_ref[rows, cols] = total.astype(BF16)
        return carry

    lax.fori_loop(0, found, gather, 0)
    items.wait()
    own.wait()


def first_call(tile_user, tile_item, tile_count, tiles, item_emb, user_emb):
    items, slots = item_emb.shape[0], tiles.shape[0]
    users = user_emb.shape[0]
    blocks = (users // BLOCK) * (items // BLOCK)
    inputs = (tile_user, tile_item, tiles, item_emb, user_emb)
    return pl.pallas_call(
        first_kernel,
        out_shape=(
            jax.ShapeDtypeStruct((users, items), BF16),
            jax.ShapeDtypeStruct((items, DIM), BF16),
            jax.ShapeDtypeStruct((users, DIM), BF16),
        ),
        in_specs=[SMEM] + [HBM] * 5,
        out_specs=(VMEM, VMEM, VMEM),
        scratch_shapes=[
            pltpu.SMEM((slots,), jnp.int32),
            pltpu.SMEM((slots,), jnp.int32),
            pltpu.SMEM((blocks,), jnp.int32),
            pltpu.SMEM((slots + 1,), jnp.int32),
            pltpu.SMEM((slots + 1,), jnp.int32),
            pltpu.VMEM((slots + 1, BLOCK, BLOCK), BF16),
            pltpu.SemaphoreType.DMA((5,)),
        ],
        compiler_params=PARAMS,
        name="first",
    )(tile_count, *(pltpu.with_memory_space_constraint(x, pltpu.HBM) for x in inputs))


def part_kernel(r_ref, item_ref, part_ref):
    part = jnp.dot(r_ref[...], item_ref[...], preferred_element_type=F32)
    part_ref[...] = part.astype(BF16)


def part_call(r, item_emb):
    return pl.pallas_call(
        part_kernel,
        out_shape=jax.ShapeDtypeStruct((r.shape[0], DIM), BF16),
        in_specs=[VMEM, VMEM],
        out_specs=VMEM,
        compiler_params=PARAMS,
        name="part",
    )(r, item_emb)


def back_kernel(r_ref, user_ref, keep_ref, send_ref, two_ref):
    back = lax.dot_general(r_ref[...], user_ref[...], FIRST_DIMS, preferred_element_type=F32)
    two_ref[...] = back.astype(BF16).reshape(two_ref.shape)
    core = lax.axis_index("core")
    keep_ref[...] = two_ref[core]
    send_ref[...] = two_ref[1 - core]


def back_call(r, user_emb):
    piece = jax.ShapeDtypeStruct((GROUP, r.shape[1] // CORE // GROUP, DIM), BF16)
    return pl.pallas_call(
        back_kernel,
        out_shape=(piece, piece),
        in_specs=[VMEM, VMEM],
        out_specs=(VMEM, VMEM),
        scratch_shapes=[pltpu.VMEM((CORE,) + piece.shape, BF16)],
        compiler_params=PARAMS,
        name="back",
    )(r, user_emb)


def join_kernel(keep_ref, sent_ref, out_ref):
    other = sent_ref[1 - lax.axis_index("core")].astype(F32)
    out_ref[...] = (keep_ref[...].astype(F32) + other).astype(BF16)


def join_call(keep, sent):
    return pl.pallas_call(
        join_kernel,
        out_shape=jax.ShapeDtypeStruct(keep.shape, BF16),
        in_specs=[VMEM, VMEM],
        out_specs=VMEM,
        compiler_params=PARAMS,
        name="join",
    )(keep, sent)


def second_kernel(r_ref, parts_ref, one_hbm, keep_ref, send_ref, two_ref, one_ref, sem):
    total = parts_ref[0].astype(F32)
    for k in range(1, parts_ref.shape[0]):
        total += parts_ref[k].astype(F32)
    one = total.astype(BF16)
    one_ref[...] = one
    copy = pltpu.make_async_copy(one_ref, one_hbm, sem)
    copy.start()
    back = lax.dot_general(r_ref[...], one, FIRST_DIMS, preferred_element_type=F32)
    back = back.reshape(ZH, ZL, Y, CORE, 8, DIM)
    for zl in range(ZL):
        for y in range(Y):
            for c in range(CORE):
                rows = jnp.concatenate([back[zh, zl, y, c] for zh in range(ZH)], axis=0)
                two_ref[c, zl * Y + y] = rows.astype(BF16)
    core = lax.axis_index("core")
    keep_ref[...] = two_ref[core]
    send_ref[...] = two_ref[1 - core]
    copy.wait()


def second_call(r, parts):
    users, items = r.shape
    piece = jax.ShapeDtypeStruct((GROUP, items // CORE // GROUP, DIM), BF16)
    return pl.pallas_call(
        second_kernel,
        out_shape=(pltpu.HBM((users, DIM), BF16), piece, piece),
        in_specs=[VMEM, VMEM],
        out_specs=(HBM, VMEM, VMEM),
        scratch_shapes=[
            pltpu.VMEM((CORE,) + piece.shape, BF16),
            pltpu.VMEM((users, DIM), BF16),
            pltpu.SemaphoreType.DMA,
        ],
        compiler_params=PARAMS,
        name="second",
    )(r, parts)


def spread_kernel(got_ref, keep_ref, sent_ref, out_ref):
    total = got_ref[0].astype(F32)
    for k in range(1, got_ref.shape[0]):
        total += got_ref[k].astype(F32)
    total = total.astype(BF16)
    for k in range(out_ref.shape[0]):
        out_ref[k, 0] = total
    other = sent_ref[1 - lax.axis_index("core")].astype(F32)
    out_ref[:, 1] = (keep_ref[...].astype(F32) + other).astype(BF16)


def spread_call(got, keep, sent):
    return pl.pallas_call(
        spread_kernel,
        out_shape=jax.ShapeDtypeStruct((GROUP, 2) + got.shape[1:], BF16),
        in_specs=[VMEM, VMEM, VMEM],
        out_specs=VMEM,
        compiler_params=PARAMS,
        name="spread",
    )(got, keep, sent)


def third_kernel(r_ref, one_ref, emb_ref, back_ref, part_ref, out_ref, two_ref):
    part = jnp.dot(r_ref[...], one_ref[...], preferred_element_type=F32)
    part_ref[...] = part.astype(BF16)
    two_ref[...] = back_ref[...].astype(F32).sum(axis=0).astype(BF16)
    block = (lax.axis_index("zh") * ZL + lax.axis_index("zl")) * Y + lax.axis_index("y")
    rows = pl.ds(pl.multiple_of(block * 16, 16), 16)
    pair = one_ref[rows].astype(F32) + emb_ref[rows].astype(F32)
    mine = jnp.where(lax.axis_index("core") == 0, pair[:8], pair[8:])
    out_ref[...] = mine


def third_call(r, item_one, item_emb, back):
    users, items = r.shape
    return pl.pallas_call(
        third_kernel,
        out_shape=(
            jax.ShapeDtypeStruct((users, DIM), BF16),
            jax.ShapeDtypeStruct((8, DIM), F32),
            jax.ShapeDtypeStruct(back.shape[1:], BF16),
        ),
        in_specs=[VMEM] * 4,
        out_specs=(VMEM, VMEM, VMEM),
        compiler_params=PARAMS,
        name="third",
    )(r, item_one, item_emb, back)


def last_kernel(user_ref, one_ref, parts_ref, base_ref, two_ref, user_out_ref, item_out_ref):
    total = user_ref[...].astype(F32) + one_ref[...].astype(F32)
    for k in range(parts_ref.shape[0]):
        total += parts_ref[k].astype(F32)
    user_out_ref[...] = (total / 3.0).astype(BF16)
    two = two_ref[...].astype(F32).sum(axis=0)
    item_out_ref[...] = ((base_ref[...] + two) / 3.0).astype(BF16)


def last_call(user_emb, user_one, parts, base, two):
    return pl.pallas_call(
        last_kernel,
        out_shape=(
            jax.ShapeDtypeStruct(user_emb.shape, BF16),
            jax.ShapeDtypeStruct(base.shape, BF16),
        ),
        in_specs=[VMEM] * 5,
        out_specs=(VMEM, VMEM),
        compiler_params=PARAMS,
        name="last",
    )(user_emb, user_one, parts, base, two)


def swap(x, axis):
    return lax.all_to_all(x, axis, 0, 0, tiled=True)


def add_up(x):
    return x.astype(F32).sum(axis=0)


def per_device(tiles, tile_user, tile_item, tile_count, user_emb, item_emb):
    r, items, own = first_call(tile_user, tile_item, tile_count, tiles, item_emb, user_emb)
    keep, send = back_call(r, own)
    chip = join_call(keep, lax.all_gather(send, "core", axis=0))
    chip, items = lax.optimization_barrier((chip, items))
    got = swap(chip, ("zl", "y"))
    part = part_call(r, items)
    near = lax.all_gather(part, "item", axis=0, axis_index_groups=[[0, 1], [2, 3]])
    pair = add_up(near).astype(BF16)

    got, pair = lax.optimization_barrier((got, pair))
    rows = add_up(got).astype(BF16)
    wide = jnp.broadcast_to(rows[None], (ZH,) + rows.shape)
    wide, pair = lax.optimization_barrier((wide, pair))
    got = swap(wide, "zh")
    parts = lax.all_gather(pair, "item", axis=0, axis_index_groups=[[0, 3], [1, 2]])
    user_one, keep, send = second_call(r, parts)
    sent = lax.all_gather(send, "core", axis=0)
    got = swap(spread_call(got, keep, sent), ("zl", "y"))

    half, back = got[:, 0], got[:, 1]
    item_one = lax.all_gather(half.reshape(-1, DIM), "core", axis=0, tiled=True)
    part, base, two = third_call(r, item_one, item_emb, back)
    two = swap(two.reshape(ZH, -1, DIM), "zh")
    parts = lax.all_gather(part, "item", axis=0)
    return last_call(user_emb, user_one, parts, base, two)


def solution(mesh):
    fine = Mesh(mesh.devices.reshape(ZH, ZL, Y, CORE, -1), AXES + ("item",))
    every = P(AXES + ("item",))
    in_specs = (every, every, every, every, P(AXES, None), P("item", None))
    out_specs = (P(AXES, None), P(("item",) + AXES, None))
    return jax.shard_map(
        per_device, mesh=fine, in_specs=in_specs, out_specs=out_specs, check_vma=False
    )
```
